32 devices in a mesh: groups: 2 (over y), shard: 16 (over z, x, core).
Axes of the slice: x: 2, y: 2, z: 4, core: 2. Of those that a mesh axis runs over, the one named last changes fastest.
Arguments:
- tokens: bfloat16 [4096, 8192], P(('groups', 'shard')), parts along dimension 0, may hold values from -6 to 6
- base_weight: bfloat16 [8192, 1024], P('shard'), may hold values from -0.0625 to 0.0625
- adapter_ids: int32 [4096, 1], P(('groups', 'shard')), parts along dimension 0, may hold values from 0 to 7; in each aligned block of 128 rows (0 to 127, 128 to 255, ...) at most 17 rows name the same one
- adapter_ranks: int32 [16], P('groups'), parts along dimension 0, may hold values from 16 to 128, as said below
- adapter_owner: int32 [16], P('groups'), parts along dimension 0, may hold values from 0 to 15, as said below
- adapter_down: bfloat16 [32, 8192, 128], P(('groups', 'shard')), parts along dimension 0, may hold values from -0.0625 to 0.0625
- adapter_up: bfloat16 [32, 128, 1024], P(('groups', 'shard')), parts along dimension 0, may hold values from -0.5 to 0.5
- grad_output: bfloat16 [4096, 1024], P(('groups', 'shard')), parts along dimension 0, may hold values from -0.5 to 0.5
Outputs:
- projected: bfloat16 [4096, 1024], P(('groups', 'shard')), parts along dimension 0
- grad_down: float32 [32, 8192, 128], P(('groups', 'shard')), parts along dimension 0
- grad_up: float32 [32, 128, 1024], P(('groups', 'shard')), parts along dimension 0
The draws below stay inside these ranges and needn't reach their ends.
There are 2 independent parts, one for each index of `groups`. The reference program is written for one: setup_inputs(seed, part) draws one part's arguments, and reference() takes and returns one part's arrays. A program takes and returns all parts, laid end to end along the dimension named above; an argument that names none is the same for every part. Nothing has to cross between parts.
Inputs may be any that keep to these rules, and one draw needn't show every extreme that they name: `adapter_ids`: the 128 tokens of one device name one adapter at most 17 times, and some adapter is named that often. `adapter_ranks`: each rank is a multiple of 16; both 16 and 128 occur. `adapter_owner`: adapters are held by distinct devices; devices 0 and 15 hold one each.
All inputs are finite; a program needn't handle non-finite values.
Results may differ from the reference program's by a relative error of at most 0.0034.
Values may be sent and summed in bfloat16 or wider, within the bound.
A program may use at most 128 MiB of HBM per device.

```python
import math
import jax
import jax.numpy as jnp
import numpy as np
from jax import lax

D = 8192
VALUE_WIDTH = 1024
RMAX = 128
TOK_DEV = 128
TOKEN_COUNT = 2048
ADAPTERS = 8
CAP = 17
N_SHARD = 16


def draw_adapter_ranks(key, part):
    key = jax.random.fold_in(key, 11)
    first, second = jax.random.split(key)
    levels = 16 * jax.random.randint(first, (ADAPTERS,), 1, RMAX // 16 + 1)
    order = jax.random.permutation(second, ADAPTERS)
    levels = levels.at[order[0]].set(RMAX).at[order[1]].set(16)
    return levels.astype(jnp.int32)


def draw_adapter_owner(key, part):
    key = jax.random.fold_in(key, 23)
    first, second = jax.random.split(key)
    others = jax.random.permutation(first, N_SHARD - 2) + 1
    chosen = jnp.concatenate([jnp.array([0, N_SHARD - 1], jnp.int32), others[:ADAPTERS - 2].astype(jnp.int32)])
    order = jax.random.permutation(second, ADAPTERS)
    return chosen[order].astype(jnp.int32)


def steps_of(own_key, dims, cuts, least, top_value):
    loudness, own = 1.0, jax.random.fold_in(own_key, 6)
    for dim, parts in cuts:
        heights = jnp.exp(jax.random.uniform(jax.random.fold_in(own, dim), (parts,), jnp.float32, least / len(cuts), top_value / len(cuts)))
        loudness = loudness * jnp.repeat(heights, dims[dim] // parts).reshape([-1 if axis == dim else 1 for axis in range(len(dims))])
    return loudness


def shared_out(key, own, number, rows, count, top, bound, slope):
    ranking = jax.random.permutation(key, count)
    packed, common = load_shares(count, rows * top, bound, slope, True), load_shares(count, rows * top, bound, slope, False)
    places = jnp.arange(count)

    def named(tallies, rotation):
        used = int((tallies > 0).sum())
        fixed = max(1, used // 4)
        moved = fixed + (places - fixed + rotation * (used - fixed)) % max(1, count - fixed)
        return jnp.zeros((count,), jnp.int32).at[ranking[jnp.where(places < fixed, places, moved)]].set(jnp.asarray(tallies, jnp.int32))

    tallies = jnp.where(number % 4 == 0, named(packed, number // 4), named(common, number - number // 4 - 1))
    mixed = jax.random.permutation(jax.random.fold_in(own, 3), count)
    giver, receiver = mixed[0:count // 2 * 2:2], mixed[1:count // 2 * 2:2]
    slack = jnp.minimum(tallies[giver] - 1, bound - tallies[receiver]) // 2
    slack = jnp.where((giver == ranking[0]) | (receiver == ranking[0]) | (tallies[receiver] == 0), 0, jnp.maximum(slack, 0))
    moved = jax.random.randint(jax.random.fold_in(own, 4), (count // 2,), 0, 1 << 20) % (slack + 1)
    tallies = tallies.at[giver].add(-moved).at[receiver].add(moved)
    labels = jnp.searchsorted(jnp.cumsum(tallies), jnp.arange(rows * top), side="right").astype(jnp.int32)
    grid = labels.reshape(top, rows).T
    grid = grid[jax.random.permutation(jax.random.fold_in(own, 1), rows)]
    rotation = jax.random.randint(jax.random.fold_in(own, 2), (rows, 1), 0, top)
    return jnp.take_along_axis(grid, (jnp.arange(top)[None, :] + rotation) % top, axis=1)


def load_shares(number_of, total, limit, slope, full):
    portions = [(1 << 20) // math.isqrt(grade ** slope) + 1 for grade in range(1, number_of + 1)]
    largest = limit if full else min(limit, max(-(-total // number_of), total * portions[0] // sum(portions)))
    least = 1 if total - largest >= number_of - 1 else 0
    given, rest = [largest] + [least] * (number_of - 1), total - largest - least * (number_of - 1)
    while rest > 0:
        candidates = [i for i in range(1, number_of) if given[i] < largest] or [i for i in range(1, number_of) if given[i] < limit]
        whole, budget = sum([portions[i] for i in candidates]), rest
        for i in candidates:
            addition = min(limit - given[i], max(1, budget * portions[i] // whole), rest)
            given[i] = given[i] + addition
            rest = rest - addition
    return np.array(given)


def bell_draw(own_key, shape, deviation, bound, cuts=(), held_as=jnp.bfloat16):
    drawn = jax.random.normal(own_key, shape, jnp.float32) * deviation
    if len(cuts) > 0:
        drawn = steps_of(own_key, shape, cuts, -0.22, 0.18) * drawn
    return jnp.clip(drawn, min=-bound, max=bound).astype(held_as)


def setup_inputs(seed: int = 0, part: int = 0) -> dict:
    key_list = jax.random.split(jax.random.key(seed), 9)
    own_keys = jax.random.split(jax.random.fold_in(key_list[8], part), 9)
    tokens = bell_draw(own_keys[0], (TOKEN_COUNT, D), 1.0, 6.0, ((0, 16),))
    base_weight = bell_draw(key_list[1], (D, VALUE_WIDTH), D ** -0.5, 0.0625, ((0, 16),))
    adapter_ids_keys = jax.random.split(jax.random.fold_in(own_keys[2], 1), TOKEN_COUNT // TOK_DEV)
    adapter_ids_turns = jax.random.permutation(jax.random.fold_in(own_keys[2], 3), TOKEN_COUNT // TOK_DEV)
    adapter_ids = jax.vmap(lambda own, number: shared_out(jax.random.fold_in(own_keys[2], 2), own, number, TOK_DEV, ADAPTERS, 1, CAP, 2))(adapter_ids_keys, adapter_ids_turns).reshape((TOKEN_COUNT, 1))
    adapter_ranks = draw_adapter_ranks(jax.random.fold_in(jax.random.fold_in(key_list[8], part), 71), part)
    adapter_owner = draw_adapter_owner(jax.random.fold_in(jax.random.fold_in(key_list[8], part), 71), part)
    adapter_down = bell_draw(own_keys[5], (N_SHARD, D, RMAX), D ** -0.5, 0.0625, ((0, 16),))
    adapter_up = bell_draw(own_keys[6], (N_SHARD, RMAX, VALUE_WIDTH), RMAX ** -0.5, 0.5, ((0, 16),))
    grad_output = bell_draw(own_keys[7], (TOKEN_COUNT, VALUE_WIDTH), 0.0625, 0.5, ((0, 16),))
    return dict(tokens=tokens, base_weight=base_weight, adapter_ids=adapter_ids, adapter_ranks=adapter_ranks, adapter_owner=adapter_owner, adapter_down=adapter_down, adapter_up=adapter_up, grad_output=grad_output)


def reference(tokens, base_weight, adapter_ids, adapter_ranks, adapter_owner, adapter_down, adapter_up, grad_output):
    frozen_output = jnp.dot(tokens, base_weight, preferred_element_type=jnp.float32)
    ids_flat = adapter_ids[:, 0]
    most_rows = N_SHARD * CAP
    tokens_pad = jnp.concatenate([tokens, jnp.zeros((1, D), tokens.dtype)], axis=0)
    grads_pad = jnp.concatenate([grad_output, jnp.zeros((1, VALUE_WIDTH), grad_output.dtype)], axis=0)
    columns = jnp.arange(RMAX, dtype=jnp.int32)

    def per_adapter(adapter):
        selected_rows = jnp.nonzero(ids_flat == adapter, size=most_rows, fill_value=TOKEN_COUNT)[0].astype(jnp.int32)
        rows = tokens_pad[selected_rows]
        grads = grads_pad[selected_rows]
        holder = adapter_owner[adapter]
        down = adapter_down[holder]
        upper = adapter_up[holder]
        rank_now = adapter_ranks[adapter]
        scale = 32.0 / rank_now.astype(jnp.float32)
        keep = columns < rank_now
        hidden = jnp.where(keep[None, :], jnp.dot(rows, down, preferred_element_type=jnp.float32), 0.0).astype(jnp.bfloat16)
        lowrank_update = (scale * jnp.dot(hidden, upper, preferred_element_type=jnp.float32)).astype(jnp.bfloat16)
        back = lax.dot_general(grads, upper, (((1,), (1,)), ((), ())), preferred_element_type=jnp.float32)
        low = jnp.where(keep[None, :], scale * back, 0.0).astype(jnp.bfloat16)
        grad_d = lax.dot_general(rows, low, (((0,), (0,)), ((), ())), preferred_element_type=jnp.float32)
        grad_u = scale * lax.dot_general(hidden, grads, (((0,), (0,)), ((), ())), preferred_element_type=jnp.float32)
        return selected_rows, lowrank_update, grad_d, grad_u

    selected_rows, lowrank_update, grad_d, grad_u = lax.map(per_adapter, jnp.arange(ADAPTERS, dtype=jnp.int32))
    lowrank_branch = jnp.zeros((TOKEN_COUNT + 1, VALUE_WIDTH), jnp.float32).at[selected_rows.reshape(-1)].set(lowrank_update.reshape(-1, VALUE_WIDTH).astype(jnp.float32))[:TOKEN_COUNT]
    projected = (frozen_output + lowrank_branch).astype(jnp.bfloat16)
    grad_down = jnp.zeros((N_SHARD, D, RMAX), jnp.float32).at[adapter_owner].set(grad_d)
    grad_up = jnp.zeros((N_SHARD, RMAX, VALUE_WIDTH), jnp.float32).at[adapter_owner].set(grad_u)
    return projected, grad_down, grad_up
```

```python
import functools

import jax
import jax.numpy as jnp
from jax import lax
from jax.experimental import pallas as pl
from jax.experimental.pallas import tpu as pltpu
from jax.sharding import PartitionSpec as P

MESH = pl.DeviceIdType.MESH
QUAD = 4


def remote(src, dst, send, recv, to):
    return pltpu.make_async_remote_copy(
        src_ref=src, dst_ref=dst, send_sem=send, recv_sem=recv,
        device_id={"shard": to}, device_id_type=MESH,
    )


def greet_all(n, me):
    barrier = pltpu.get_barrier_semaphore()

    @pl.loop(1, n)
    def _(k):
        pl.semaphore_signal(
            barrier, inc=1, device_id={"shard": lax.rem(me + k, n)}, device_id_type=MESH
        )

    pl.semaphore_wait(barrier, n - 1)


def exchange_copy(n, me, k, src, dst, send, recv):
    to = lax.rem(me + k, n)
    return remote(src.at[to], dst.at[me], send.at[k], recv.at[k], to)


def start_exchange(n, me, pairs, send, recv, own):
    for i, (src, dst) in enumerate(pairs):
        pltpu.make_async_copy(src.at[me], dst.at[me], own.at[i]).start()

    @pl.loop(1, n)
    def _(k):
        for i, (src, dst) in enumerate(pairs):
            exchange_copy(n, me, k, src, dst, send.at[i], recv.at[i]).start()


def finish_exchange(n, me, pairs, send, recv, own):
    for i, (src, dst) in enumerate(pairs):
        pltpu.make_async_copy(src.at[me], dst.at[me], own.at[i]).wait()

    @pl.loop(1, n)
    def _(k):
        for i, (src, dst) in enumerate(pairs):
            exchange_copy(n, me, k, src, dst, send.at[i], recv.at[i]).wait()


def back_kernel(n, count, *refs):
    pairs = list(zip(refs[:count], refs[count:2 * count]))
    send, recv, own = refs[2 * count:]
    me = lax.axis_index("shard")
    greet_all(n, me)
    start_exchange(n, me, pairs, send, recv, own)
    finish_exchange(n, me, pairs, send, recv, own)


def forward_kernel(n, count, *refs):
    ins, outs = refs[:count], refs[count + 2:2 * count + 2]
    quarters_ref, weight_ref = refs[count:count + 2]
    base_ref = refs[2 * count + 2]
    (quad_tokens, weights, partial, partial_in, send, recv, own,
     w_right, w_left, w_recv, t_send, t_recv, p_send, p_recv, local_sem) = refs[2 * count + 3:]
    pairs = list(zip(ins, outs))
    me = lax.axis_index("shard")
    lines = n // QUAD
    row, col = me // QUAD, lax.rem(me, QUAD)
    depth = weight_ref.shape[0]

    def block(j):
        return weights.at[pl.ds(pl.multiple_of(j * depth, depth), depth)]

    def to_right(j):
        return remote(block(j), block(j), w_right.at[j], w_recv.at[j], me + QUAD)

    def to_left(j):
        return remote(block(j), block(j), w_left.at[j], w_recv.at[j], me - QUAD)

    def token_copy(k):
        other = lax.rem(col + k, QUAD)
        return remote(quarters_ref.at[other], quad_tokens.at[col], t_send.at[k], t_recv.at[k],
                      row * QUAD + other)

    def partial_copy(k):
        other = lax.rem(col + k, QUAD)
        return remote(partial.at[other], partial_in.at[col], p_send.at[k], p_recv.at[k],
                      row * QUAD + other)

    own_weight = pltpu.make_async_copy(weight_ref, block(row), local_sem.at[0])
    own_tokens = pltpu.make_async_copy(quarters_ref.at[col], quad_tokens.at[col], local_sem.at[1])
    own_weight.start()
    own_tokens.start()
    greet_all(n, me)
    own_weight.wait()

    @pl.when(row < lines - 1)
    def _():
        to_right(row).start()

    @pl.when(row > 0)
    def _():
        to_left(row).start()

    for k in range(1, QUAD):
        token_copy(k).start()
    start_exchange(n, me, pairs, send, recv, own)

    @pl.loop(1, lines)
    def _(t):
        @pl.when(row - t >= 0)
        def _():
            to_right(row - t).wait_recv()

            @pl.when(row < lines - 1)
            def _():
                to_right(row - t).start()

        @pl.when(row + t <= lines - 1)
        def _():
            to_left(row + t).wait_recv()

            @pl.when(row > 0)
            def _():
                to_left(row + t).start()

    own_tokens.wait()
    for k in range(1, QUAD):
        token_copy(k).wait()
    for k in (1, 2, 3, 0):
        other = lax.rem(col + k, QUAD)
        partial[other] = jnp.dot(
            quad_tokens[other], weights[...], preferred_element_type=jnp.float32
        )
        if k > 0:
            partial_copy(k).start()
    total = partial[col]
    for k in range(1, QUAD):
        partial_copy(k).wait()
        total = total + partial_in[lax.rem(col - k + QUAD, QUAD)]
    base_ref[...] = total

    @pl.when(row < lines - 1)
    def _():
        @pl.loop(0, row + 1)
        def _(j):
            to_right(j).wait_send()

    @pl.when(row > 0)
    def _():
        @pl.loop(row, lines)
        def _(j):
            to_left(j).wait_send()

    finish_exchange(n, me, pairs, send, recv, own)


def exchange_sems(n, count):
    return [pltpu.SemaphoreType.DMA((count, n)), pltpu.SemaphoreType.DMA((count, n)),
            pltpu.SemaphoreType.DMA((count,))]


ANY = pl.BlockSpec(memory_space=pl.ANY)
VMEM = pl.BlockSpec(memory_space=pltpu.VMEM)


def forward(n, sends, quarters, base_weight):
    count = len(sends)
    lines = n // QUAD
    rows, quarter = quarters.shape[1:]
    wide = base_weight.shape[1]
    dma = pltpu.SemaphoreType.DMA
    return pl.pallas_call(
        functools.partial(forward_kernel, n, count),
        out_shape=[jax.ShapeDtypeStruct(s.shape, s.dtype) for s in sends]
        + [jax.ShapeDtypeStruct((rows, wide), jnp.float32)],
        in_specs=[ANY] * (count + 2),
        out_specs=[ANY] * count + [VMEM],
        scratch_shapes=[
            pltpu.VMEM((QUAD, rows, quarter), jnp.bfloat16),
            pltpu.VMEM((quarter, wide), jnp.bfloat16),
            pltpu.VMEM((QUAD, rows, wide), jnp.float32),
            pltpu.VMEM((QUAD, rows, wide), jnp.float32),
        ] + exchange_sems(n, count) + [dma((lines,))] * 3 + [dma((QUAD,))] * 4 + [dma((2,))],
        compiler_params=pltpu.CompilerParams(
            collective_id=0, has_side_effects=True, vmem_limit_bytes=40 * 2**20
        ),
    )(*sends, quarters, base_weight)


def back(n, sends):
    count = len(sends)
    return pl.pallas_call(
        functools.partial(back_kernel, n, count),
        out_shape=[jax.ShapeDtypeStruct(s.shape, s.dtype) for s in sends],
        in_specs=[ANY] * count,
        out_specs=[ANY] * count,
        scratch_shapes=exchange_sems(n, count),
        compiler_params=pltpu.CompilerParams(collective_id=1, has_side_effects=True),
    )(*sends)


def packed(x):
    n, cells = x.shape
    return jnp.pad(x, ((0, 0), (0, -cells % 2048))).reshape(n, 16, -1)


def unpacked(x, cells):
    return x.reshape(x.shape[0], -1)[:, :cells]


def local(
    tokens,
    base_weight,
    adapter_ids,
    adapter_ranks,
    adapter_owner,
    adapter_down,
    adapter_up,
    grad_output,
):
    n = lax.axis_size("shard")
    here_index = lax.axis_index("shard")
    rows, width = tokens.shape
    wide = base_weight.shape[1]
    rank_max = adapter_down.shape[2]
    adapters = adapter_owner.shape[0]
    capacity = (rows + adapters - 1) // adapters + 1
    whole = capacity // 16 * 16
    rest = capacity - whole
    lines = n // QUAD
    both = width + wide
    bf16, f32 = jnp.bfloat16, jnp.float32

    ids = adapter_ids[:, 0]
    match = ids[:, None] == jnp.arange(adapters, dtype=jnp.int32)[None, :]
    target = jnp.sum(jnp.where(match, adapter_owner[None, :], 0), axis=1)
    same = ids[:, None] == ids[None, :]
    earlier = jnp.arange(rows)[:, None] > jnp.arange(rows)[None, :]
    position = jnp.sum((same & earlier).astype(jnp.int32), axis=1)

    joined = jnp.concatenate([tokens, grad_output], axis=1)
    sends, picks = [], []
    if whole:
        slot = jnp.where(position < whole, target * whole + position, -1)
        pick = (jnp.arange(n * whole)[:, None] == slot[None, :]).astype(bf16)
        picks.append(pick)
        sends.append(
            jnp.dot(pick, joined, preferred_element_type=bf16).reshape(n, whole, both)
        )
    if rest:
        slot = jnp.where(position >= whole, target * rest + position - whole, -1)
        pick = (jnp.arange(n * rest)[:, None] == slot[None, :]).astype(bf16)
        picks.append(pick)
        sends.append(packed(
            jnp.dot(pick, joined, preferred_element_type=bf16).reshape(n, rest * both)
        ))
    quarters = tokens.reshape(rows, lines, QUAD, -1).transpose(2, 0, 1, 3).reshape(QUAD, rows, -1)

    got = forward(n, sends, quarters, base_weight)
    base = got[-1]
    blocks = []
    if whole:
        blocks.append(got[0].reshape(n * whole, both))
    if rest:
        blocks.append(unpacked(got[-2], rest * both).reshape(n * rest, both))

    rank_here = jnp.sum(jnp.where(adapter_owner == here_index, adapter_ranks, 0))
    rank_safe = jnp.where(rank_here > 0, rank_here, 16)
    scale = 32.0 / rank_safe.astype(f32)
    keep = jnp.arange(rank_max, dtype=jnp.int32) < rank_here
    block = jnp.concatenate(blocks, axis=0)
    token_block, grad_block = block[:, :width], block[:, width:]
    hidden = jnp.where(
        keep[None, :],
        jnp.dot(token_block, adapter_down[0], preferred_element_type=f32),
        0.0,
    ).astype(bf16)
    update = (scale * jnp.dot(hidden, adapter_up[0], preferred_element_type=f32)).astype(bf16)
    sends = []
    if whole:
        sends.append(update[:n * whole].reshape(n, whole, wide))
    if rest:
        sends.append(packed(update[n * whole:].reshape(n, rest * wide)))
    got = back(n, sends)
    blocks = []
    if whole:
        blocks.append(got[0].reshape(n * whole, wide))
    if rest:
        blocks.append(unpacked(got[-1], rest * wide).reshape(n * rest, wide))
    branch = sum(
        lax.dot_general(p, b, (((0,), (0,)), ((), ())), preferred_element_type=f32)
        for p, b in zip(picks, blocks)
    )
    projected = (base + branch).astype(bf16)
    grad_low = lax.dot_general(
        grad_block, adapter_up[0], (((1,), (1,)), ((), ())), preferred_element_type=f32
    )
    low = jnp.where(keep[None, :], scale * grad_low, 0.0).astype(bf16)
    grad_down = lax.dot_general(
        token_block, low, (((0,), (0,)), ((), ())), preferred_element_type=f32
    )
    grad_up = scale * lax.dot_general(
        hidden, grad_block, (((0,), (0,)), ((), ())), preferred_element_type=f32
    )
    return (projected, grad_down[None], grad_up[None])


def solution(mesh):
    in_specs = (
        P(("groups", "shard"), None),
        P("shard", None),
        P(("groups", "shard"), None),
        P("groups"),
        P("groups"),
        P(("groups", "shard"), None, None),
        P(("groups", "shard"), None, None),
        P(("groups", "shard"), None),
    )
    out_specs = (
        P(("groups", "shard"), None),
        P(("groups", "shard"), None, None),
        P(("groups", "shard"), None, None),
    )
    return jax.shard_map(local, mesh=mesh, in_specs=in_specs, out_specs=out_specs, check_vma=False)
```

```python
import functools

import jax
import jax.numpy as jnp
from jax import lax
from jax.experimental import pallas as pl
from jax.experimental.pallas import tpu as pltpu
from jax.sharding import PartitionSpec as P

MESH = pl.DeviceIdType.MESH
QUAD = 4


def remote(src, dst, send, recv, to):
    return pltpu.make_async_remote_copy(
        src_ref=src, dst_ref=dst, send_sem=send, recv_sem=recv,
        device_id={"shard": to}, device_id_type=MESH,
    )


def greet_all(n, me):
    barrier = pltpu.get_barrier_semaphore()

    @pl.loop(1, n)
    def _(k):
        pl.semaphore_signal(
            barrier, inc=1, device_id={"shard": lax.rem(me + k, n)}, device_id_type=MESH
        )

    pl.semaphore_wait(barrier, n - 1)


def exchange_copy(n, me, k, src, dst, send, recv):
    to = lax.rem(me + k, n)
    return remote(src.at[to], dst.at[me], send.at[k], recv.at[k], to)


def start_exchange(n, me, pairs, send, recv, own):
    for i, (src, dst) in enumerate(pairs):
        pltpu.make_async_copy(src.at[me], dst.at[me], own.at[i]).start()

    @pl.loop(1, n)
    def _(step):
        k = lax.rem(step * (n // 2 - 1), n)
        for i, (src, dst) in enumerate(pairs):
            exchange_copy(n, me, k, src, dst, send.at[i], recv.at[i]).start()


def finish_exchange(n, me, pairs, send, recv, own):
    for i, (src, dst) in enumerate(pairs):
        pltpu.make_async_copy(src.at[me], dst.at[me], own.at[i]).wait()

    @pl.loop(1, n)
    def _(k):
        for i, (src, dst) in enumerate(pairs):
            exchange_copy(n, me, k, src, dst, send.at[i], recv.at[i]).wait()


def back_kernel(n, count, *refs):
    pairs = list(zip(refs[:count], refs[count:2 * count]))
    send, recv, own = refs[2 * count:]
    me = lax.axis_index("shard")
    greet_all(n, me)
    start_exchange(n, me, pairs, send, recv, own)
    finish_exchange(n, me, pairs, send, recv, own)


def forward_kernel(n, count, *refs):
    ins, outs = refs[:count], refs[count + 2:2 * count + 2]
    quarters_ref, weight_ref = refs[count:count + 2]
    base_ref = refs[2 * count + 2]
    (quad_tokens, weights, partial, partial_in, send, recv, own,
     w_right, w_left, w_recv, t_send, t_recv, p_send, p_recv, local_sem) = refs[2 * count + 3:]
    pairs = list(zip(ins, outs))
    me = lax.axis_index("shard")
    lines = n // QUAD
    row, col = me // QUAD, lax.rem(me, QUAD)
    depth = weight_ref.shape[0]

    def block(j):
        return weights.at[pl.ds(pl.multiple_of(j * depth, depth), depth)]

    def to_right(j):
        return remote(block(j), block(j), w_right.at[j], w_recv.at[j], me + QUAD)

    def to_left(j):
        return remote(block(j), block(j), w_left.at[j], w_recv.at[j], me - QUAD)

    def token_copy(k):
        other = lax.rem(col + k, QUAD)
        return remote(quarters_ref.at[other], quad_tokens.at[col], t_send.at[k], t_recv.at[k],
                      row * QUAD + other)

    def partial_copy(k):
        other = lax.rem(col + k, QUAD)
        return remote(partial.at[other], partial_in.at[col], p_send.at[k], p_recv.at[k],
                      row * QUAD + other)

    own_weight = pltpu.make_async_copy(weight_ref, block(row), local_sem.at[0])
    own_tokens = pltpu.make_async_copy(quarters_ref.at[col], quad_tokens.at[col], local_sem.at[1])
    own_weight.start()
    own_tokens.start()
    greet_all(n, me)
    own_weight.wait()

    @pl.when(row < lines - 1)
    def _():
        to_right(row).start()

    @pl.when(row > 0)
    def _():
        to_left(row).start()

    for k in range(1, QUAD):
        token_copy(k).start()
    start_exchange(n, me, pairs, send, recv, own)

    @pl.loop(1, lines)
    def _(t):
        @pl.when(row - t >= 0)
        def _():
            to_right(row - t).wait_recv()

            @pl.when(row < lines - 1)
            def _():
                to_right(row - t).start()

        @pl.when(row + t <= lines - 1)
        def _():
            to_left(row + t).wait_recv()

            @pl.when(row > 0)
            def _():
                to_left(row + t).start()

    own_tokens.wait()
    for k in range(1, QUAD):
        token_copy(k).wait()
    for k in (1, 2, 3, 0):
        other = lax.rem(col + k, QUAD)
        partial[other] = jnp.dot(
            quad_tokens[other], weights[...], preferred_element_type=jnp.float32
        )
        if k > 0:
            partial_copy(k).start()
    total = partial[col]
    for k in range(1, QUAD):
        partial_copy(k).wait()
        total = total + partial_in[lax.rem(col - k + QUAD, QUAD)]
    base_ref[...] = total

    @pl.when(row < lines - 1)
    def _():
        @pl.loop(0, row + 1)
        def _(j):
            to_right(j).wait_send()

    @pl.when(row > 0)
    def _():
        @pl.loop(row, lines)
        def _(j):
            to_left(j).wait_send()

    finish_exchange(n, me, pairs, send, recv, own)


def exchange_sems(n, count):
    return [pltpu.SemaphoreType.DMA((count, n)), pltpu.SemaphoreType.DMA((count, n)),
            pltpu.SemaphoreType.DMA((count,))]


ANY = pl.BlockSpec(memory_space=pl.ANY)
VMEM = pl.BlockSpec(memory_space=pltpu.VMEM)


def forward(n, sends, quarters, base_weight):
    count = len(sends)
    lines = n // QUAD
    rows, quarter = quarters.shape[1:]
    wide = base_weight.shape[1]
    dma = pltpu.SemaphoreType.DMA
    return pl.pallas_call(
        functools.partial(forward_kernel, n, count),
        out_shape=[jax.ShapeDtypeStruct(s.shape, s.dtype) for s in sends]
        + [jax.ShapeDtypeStruct((rows, wide), jnp.float32)],
        in_specs=[ANY] * (count + 2),
        out_specs=[ANY] * count + [VMEM],
        scratch_shapes=[
            pltpu.VMEM((QUAD, rows, quarter), jnp.bfloat16),
            pltpu.VMEM((quarter, wide), jnp.bfloat16),
            pltpu.VMEM((QUAD, rows, wide), jnp.float32),
            pltpu.VMEM((QUAD, rows, wide), jnp.float32),
        ] + exchange_sems(n, count) + [dma((lines,))] * 3 + [dma((QUAD,))] * 4 + [dma((2,))],
        compiler_params=pltpu.CompilerParams(
            collective_id=0, has_side_effects=True, vmem_limit_bytes=40 * 2**20
        ),
    )(*sends, quarters, base_weight)


def back(n, sends):
    count = len(sends)
    return pl.pallas_call(
        functools.partial(back_kernel, n, count),
        out_shape=[jax.ShapeDtypeStruct(s.shape, s.dtype) for s in sends],
        in_specs=[ANY] * count,
        out_specs=[ANY] * count,
        scratch_shapes=exchange_sems(n, count),
        compiler_params=pltpu.CompilerParams(collective_id=1, has_side_effects=True),
    )(*sends)


def packed(x):
    n, cells = x.shape
    return jnp.pad(x, ((0, 0), (0, -cells % 2048))).reshape(n, 16, -1)


def unpacked(x, cells):
    return x.reshape(x.shape[0], -1)[:, :cells]


def local(
    tokens,
    base_weight,
    adapter_ids,
    adapter_ranks,
    adapter_owner,
    adapter_down,
    adapter_up,
    grad_output,
):
    n = lax.axis_size("shard")
    here_index = lax.axis_index("shard")
    rows, width = tokens.shape
    wide = base_weight.shape[1]
    rank_max = adapter_down.shape[2]
    adapters = adapter_owner.shape[0]
    capacity = (rows + adapters - 1) // adapters + 1
    whole = capacity // 16 * 16
    rest = capacity - whole
    lines = n // QUAD
    both = width + wide
    bf16, f32 = jnp.bfloat16, jnp.float32

    ids = adapter_ids[:, 0]
    match = ids[:, None] == jnp.arange(adapters, dtype=jnp.int32)[None, :]
    target = jnp.sum(jnp.where(match, adapter_owner[None, :], 0), axis=1)
    same = ids[:, None] == ids[None, :]
    earlier = jnp.arange(rows)[:, None] > jnp.arange(rows)[None, :]
    position = jnp.sum((same & earlier).astype(jnp.int32), axis=1)

    joined = jnp.concatenate([tokens, grad_output], axis=1)
    sends, picks = [], []
    if whole:
        slot = jnp.where(position < whole, target * whole + position, -1)
        pick = (jnp.arange(n * whole)[:, None] == slot[None, :]).astype(bf16)
        picks.append(pick)
        sends.append(
            jnp.dot(pick, joined, preferred_element_type=bf16).reshape(n, whole, both)
        )
    if rest:
        slot = jnp.where(position >= whole, target * rest + position - whole, -1)
        pick = (jnp.arange(n * rest)[:, None] == slot[None, :]).astype(bf16)
        picks.append(pick)
        sends.append(packed(
            jnp.dot(pick, joined, preferred_element_type=bf16).reshape(n, rest * both)
        ))
    depth = width // n
    quarters = jnp.stack([
        jnp.concatenate([
            tokens[:, (j * QUAD + c) * depth:(j * QUAD + c + 1) * depth] for j in range(lines)
        ], axis=1)
        for c in range(QUAD)
    ])

    got = forward(n, sends, quarters, base_weight)
    base = got[-1]
    blocks = []
    if whole:
        blocks.append(got[0].reshape(n * whole, both))
    if rest:
        blocks.append(unpacked(got[-2], rest * both).reshape(n * rest, both))

    rank_here = jnp.sum(jnp.where(adapter_owner == here_index, adapter_ranks, 0))
    rank_safe = jnp.where(rank_here > 0, rank_here, 16)
    scale = 32.0 / rank_safe.astype(f32)
    keep = jnp.arange(rank_max, dtype=jnp.int32) < rank_here
    block = jnp.concatenate(blocks, axis=0)
    token_block, grad_block = block[:, :width], block[:, width:]
    hidden = jnp.where(
        keep[None, :],
        jnp.dot(token_block, adapter_down[0], preferred_element_type=f32),
        0.0,
    ).astype(bf16)
    update = (scale * jnp.dot(hidden, adapter_up[0], preferred_element_type=f32)).astype(bf16)
    sends = []
    if whole:
        sends.append(update[:n * whole].reshape(n, whole, wide))
    if rest:
        sends.append(packed(update[n * whole:].reshape(n, rest * wide)))
    got = back(n, sends)
    blocks = []
    if whole:
        blocks.append(got[0].reshape(n * whole, wide))
    if rest:
        blocks.append(unpacked(got[-1], rest * wide).reshape(n * rest, wide))
    branch = sum(
        lax.dot_general(p, b, (((0,), (0,)), ((), ())), preferred_element_type=f32)
        for p, b in zip(picks, blocks)
    )
    projected = (base + branch).astype(bf16)
    grad_low = lax.dot_general(
        grad_block, adapter_up[0], (((1,), (1,)), ((), ())), preferred_element_type=f32
    )
    low = jnp.where(keep[None, :], scale * grad_low, 0.0).astype(bf16)
    grad_down = lax.dot_general(
        token_block, low, (((0,), (0,)), ((), ())), preferred_element_type=f32
    )
    grad_up = scale * lax.dot_general(
        hidden, grad_block, (((0,), (0,)), ((), ())), preferred_element_type=f32
    )
    return (projected, grad_down[None], grad_up[None])


def solution(mesh):
    in_specs = (
        P(("groups", "shard"), None),
        P("shard", None),
        P(("groups", "shard"), None),
        P("groups"),
        P("groups"),
        P(("groups", "shard"), None, None),
        P(("groups", "shard"), None, None),
        P(("groups", "shard"), None),
    )
    out_specs = (
        P(("groups", "shard"), None),
        P(("groups", "shard"), None, None),
        P(("groups", "shard"), None, None),
    )
    return jax.shard_map(local, mesh=mesh, in_specs=in_specs, out_specs=out_specs, check_vma=False)
```

```python
import functools

import jax
import jax.numpy as jnp
from jax import lax
from jax.experimental import pallas as pl
from jax.experimental.pallas import tpu as pltpu
from jax.sharding import PartitionSpec as P

MESH = pl.DeviceIdType.MESH
QUAD = 4


def remote(src, dst, send, recv, to):
    return pltpu.make_async_remote_copy(
        src_ref=src, dst_ref=dst, send_sem=send, recv_sem=recv,
        device_id={"shard": to}, device_id_type=MESH,
    )


def greet_all(n, me, shares=1):
    barrier = pltpu.get_barrier_semaphore()
    if shares == 2:
        pl.semaphore_signal(
            barrier, inc=1, device_id={"groups": 1 - lax.axis_index("groups"), "shard": me},
            device_id_type=MESH,
        )

    @pl.loop(1, n)
    def _(k):
        pl.semaphore_signal(
            barrier, inc=1, device_id={"shard": lax.rem(me + k, n)}, device_id_type=MESH
        )

    pl.semaphore_wait(barrier, n - 2 + shares)


def exchange_copy(n, me, k, src, dst, send, recv):
    to = lax.rem(me + k, n)
    return remote(src.at[to], dst.at[me], send.at[k], recv.at[k], to)


def start_own(me, pairs, own):
    for i, (src, dst) in enumerate(pairs):
        pltpu.make_async_copy(src.at[me], dst.at[me], own.at[i]).start()


def start_exchange(n, me, pairs, send, recv, first, last):
    @pl.loop(first, last)
    def _(step):
        k = lax.rem(step * (n // 2 - 1), n)
        for i, (src, dst) in enumerate(pairs):
            exchange_copy(n, me, k, src, dst, send.at[i], recv.at[i]).start()


def finish_exchange(n, me, pairs, send, recv, own):
    for i, (src, dst) in enumerate(pairs):
        pltpu.make_async_copy(src.at[me], dst.at[me], own.at[i]).wait()

    @pl.loop(1, n)
    def _(k):
        for i, (src, dst) in enumerate(pairs):
            exchange_copy(n, me, k, src, dst, send.at[i], recv.at[i]).wait()


def back_kernel(n, count, *refs):
    pairs = list(zip(refs[:count], refs[count:2 * count]))
    send, recv, own = refs[2 * count:]
    me = lax.axis_index("shard")
    greet_all(n, me)
    start_own(me, pairs, own)
    start_exchange(n, me, pairs, send, recv, 1, n)
    finish_exchange(n, me, pairs, send, recv, own)


def forward_kernel(n, count, shares, *refs):
    ins, outs = refs[:count], refs[count + 2:2 * count + 2]
    quarters_ref, weight_ref = refs[count:count + 2]
    base_ref = refs[2 * count + 2]
    (quad_tokens, weights, partial, partial_in, send, recv, own,
     w_right, w_left, w_recv, y_send, y_recv, t_send, t_recv, p_send, p_recv, local_sem) = refs[2 * count + 3:]
    pairs = list(zip(ins, outs))
    me = lax.axis_index("shard")
    lines = n // QUAD
    row, col = me // QUAD, lax.rem(me, QUAD)
    depth = weight_ref.shape[0]

    group = lax.axis_index("groups")
    half = depth // shares

    def block(j):
        first = j * depth + (group * half if shares == 2 else 0)
        return weights.at[pl.ds(pl.multiple_of(first, half), half)]

    def across(j):
        return pltpu.make_async_remote_copy(
            src_ref=block(j), dst_ref=block(j), send_sem=y_send.at[j], recv_sem=y_recv.at[j],
            device_id={"groups": 1 - group, "shard": me}, device_id_type=MESH,
        )

    def to_right(j):
        return remote(block(j), block(j), w_right.at[j], w_recv.at[j], me + QUAD)

    def to_left(j):
        return remote(block(j), block(j), w_left.at[j], w_recv.at[j], me - QUAD)

    def token_copy(k):
        other = lax.rem(col + k, QUAD)
        return remote(quarters_ref.at[other], quad_tokens.at[col], t_send.at[k], t_recv.at[k],
                      row * QUAD + other)

    def partial_copy(k):
        other = lax.rem(col + k, QUAD)
        return remote(partial.at[other], partial_in.at[col], p_send.at[k], p_recv.at[k],
                      row * QUAD + other)

    own_weight = pltpu.make_async_copy(
        weight_ref, weights.at[pl.ds(pl.multiple_of(row * depth, depth), depth)], local_sem.at[0]
    )
    own_tokens = pltpu.make_async_copy(quarters_ref.at[col], quad_tokens.at[col], local_sem.at[1])
    own_weight.start()
    own_tokens.start()
    greet_all(n, me, shares)
    own_weight.wait()

    @pl.when(row < lines - 1)
    def _():
        to_right(row).start()

    @pl.when(row > 0)
    def _():
        to_left(row).start()

    for k in range(1, QUAD):
        token_copy(k).start()
    start_own(me, pairs, own)
    step = -(-(n - 1) // (lines - 1))

    @pl.loop(1, lines)
    def _(t):
        start_exchange(n, me, pairs, send, recv, 1 + (t - 1) * step,
                       jnp.minimum(1 + t * step, n))

        @pl.when(row - t >= 0)
        def _():
            to_right(row - t).wait_recv()

            @pl.when(row < lines - 1)
            def _():
                to_right(row - t).start()

            if shares == 2:
                across(row - t).start()

        @pl.when(row + t <= lines - 1)
        def _():
            to_left(row + t).wait_recv()

            @pl.when(row > 0)
            def _():
                to_left(row + t).start()

            if shares == 2:
                across(row + t).start()

    if shares == 2:
        @pl.loop(0, lines)
        def _(j):
            @pl.when(j != row)
            def _():
                across(j).wait()

    own_tokens.wait()
    for k in range(1, QUAD):
        token_copy(k).wait()
    for k in (1, 2, 3, 0):
        other = lax.rem(col + k, QUAD)
        partial[other] = jnp.dot(
            quad_tokens[other], weights[...], preferred_element_type=jnp.float32
        )
        if k > 0:
            partial_copy(k).start()
    total = partial[col]
    for k in range(1, QUAD):
        partial_copy(k).wait()
        total = total + partial_in[lax.rem(col - k + QUAD, QUAD)]
    base_ref[...] = total

    @pl.when(row < lines - 1)
    def _():
        @pl.loop(0, row + 1)
        def _(j):
            to_right(j).wait_send()

    @pl.when(row > 0)
    def _():
        @pl.loop(row, lines)
        def _(j):
            to_left(j).wait_send()

    finish_exchange(n, me, pairs, send, recv, own)


def exchange_sems(n, count):
    return [pltpu.SemaphoreType.DMA((count, n)), pltpu.SemaphoreType.DMA((count, n)),
            pltpu.SemaphoreType.DMA((count,))]


ANY = pl.BlockSpec(memory_space=pl.ANY)
VMEM = pl.BlockSpec(memory_space=pltpu.VMEM)


def forward(n, sends, quarters, base_weight):
    count = len(sends)
    lines = n // QUAD
    shares = 2 if lax.axis_size("groups") == 2 and base_weight.shape[0] % 32 == 0 else 1
    rows, quarter = quarters.shape[1:]
    wide = base_weight.shape[1]
    dma = pltpu.SemaphoreType.DMA
    return pl.pallas_call(
        functools.partial(forward_kernel, n, count, shares),
        out_shape=[jax.ShapeDtypeStruct(s.shape, s.dtype) for s in sends]
        + [jax.ShapeDtypeStruct((rows, wide), jnp.float32)],
        in_specs=[ANY] * (count + 2),
        out_specs=[ANY] * count + [VMEM],
        scratch_shapes=[
            pltpu.VMEM((QUAD, rows, quarter), jnp.bfloat16),
            pltpu.VMEM((quarter, wide), jnp.bfloat16),
            pltpu.VMEM((QUAD, rows, wide), jnp.float32),
            pltpu.VMEM((QUAD, rows, wide), jnp.float32),
        ] + exchange_sems(n, count) + [dma((lines,))] * 5 + [dma((QUAD,))] * 4 + [dma((2,))],
        compiler_params=pltpu.CompilerParams(
            collective_id=0, has_side_effects=True, vmem_limit_bytes=40 * 2**20
        ),
    )(*sends, quarters, base_weight)


def back(n, sends):
    count = len(sends)
    return pl.pallas_call(
        functools.partial(back_kernel, n, count),
        out_shape=[jax.ShapeDtypeStruct(s.shape, s.dtype) for s in sends],
        in_specs=[ANY] * count,
        out_specs=[ANY] * count,
        scratch_shapes=exchange_sems(n, count),
        compiler_params=pltpu.CompilerParams(collective_id=1, has_side_effects=True),
    )(*sends)


def packed(x):
    n, cells = x.shape
    return jnp.pad(x, ((0, 0), (0, -cells % 2048))).reshape(n, 16, -1)


def unpacked(x, cells):
    return x.reshape(x.shape[0], -1)[:, :cells]


def local(
    tokens,
    base_weight,
    adapter_ids,
    adapter_ranks,
    adapter_owner,
    adapter_down,
    adapter_up,
    grad_output,
):
    n = lax.axis_size("shard")
    here_index = lax.axis_index("shard")
    rows, width = tokens.shape
    wide = base_weight.shape[1]
    rank_max = adapter_down.shape[2]
    adapters = adapter_owner.shape[0]
    capacity = (rows + adapters - 1) // adapters + 1
    whole = capacity // 16 * 16
    rest = capacity - whole
    lines = n // QUAD
    both = width + wide
    bf16, f32 = jnp.bfloat16, jnp.float32

    ids = adapter_ids[:, 0]
    match = ids[:, None] == jnp.arange(adapters, dtype=jnp.int32)[None, :]
    target = jnp.sum(jnp.where(match, adapter_owner[None, :], 0), axis=1)
    same = ids[:, None] == ids[None, :]
    earlier = jnp.arange(rows)[:, None] > jnp.arange(rows)[None, :]
    position = jnp.sum((same & earlier).astype(jnp.int32), axis=1)

    joined = jnp.concatenate([tokens, grad_output], axis=1)
    sends, picks = [], []
    if whole:
        slot = jnp.where(position < whole, target * whole + position, -1)
        pick = (jnp.arange(n * whole)[:, None] == slot[None, :]).astype(bf16)
        picks.append(pick)
        sends.append(
            jnp.dot(pick, joined, preferred_element_type=bf16).reshape(n, whole, both)
        )
    if rest:
        slot = jnp.where(position >= whole, target * rest + position - whole, -1)
        pick = (jnp.arange(n * rest)[:, None] == slot[None, :]).astype(bf16)
        picks.append(pick)
        sends.append(packed(
            jnp.dot(pick, joined, preferred_element_type=bf16).reshape(n, rest * both)
        ))
    depth = width // n
    quarters = jnp.stack([
        jnp.concatenate([
            tokens[:, (j * QUAD + c) * depth:(j * QUAD + c + 1) * depth] for j in range(lines)
        ], axis=1)
        for c in range(QUAD)
    ])

    got = forward(n, sends, quarters, base_weight)
    base = got[-1]
    blocks = []
    if whole:
        blocks.append(got[0].reshape(n * whole, both))
    if rest:
        blocks.append(unpacked(got[-2], rest * both).reshape(n * rest, both))

    rank_here = jnp.sum(jnp.where(adapter_owner == here_index, adapter_ranks, 0))
    rank_safe = jnp.where(rank_here > 0, rank_here, 16)
    scale = 32.0 / rank_safe.astype(f32)
    keep = jnp.arange(rank_max, dtype=jnp.int32) < rank_here
    block = jnp.concatenate(blocks, axis=0)
    token_block, grad_block = block[:, :width], block[:, width:]
    hidden = jnp.where(
        keep[None, :],
        jnp.dot(token_block, adapter_down[0], preferred_element_type=f32),
        0.0,
    ).astype(bf16)
    update = (scale * jnp.dot(hidden, adapter_up[0], preferred_element_type=f32)).astype(bf16)
    sends = []
    if whole:
        sends.append(update[:n * whole].reshape(n, whole, wide))
    if rest:
        sends.append(packed(update[n * whole:].reshape(n, rest * wide)))
    got = back(n, sends)
    blocks = []
    if whole:
        blocks.append(got[0].reshape(n * whole, wide))
    if rest:
        blocks.append(unpacked(got[-1], rest * wide).reshape(n * rest, wide))
    branch = sum(
        lax.dot_general(p, b, (((0,), (0,)), ((), ())), preferred_element_type=f32)
        for p, b in zip(picks, blocks)
    )
    projected = (base + branch).astype(bf16)
    grad_low = lax.dot_general(
        grad_block, adapter_up[0], (((1,), (1,)), ((), ())), preferred_element_type=f32
    )
    low = jnp.where(keep[None, :], scale * grad_low, 0.0).astype(bf16)
    grad_down = lax.dot_general(
        token_block, low, (((0,), (0,)), ((), ())), preferred_element_type=f32
    )
    grad_up = scale * lax.dot_general(
        hidden, grad_block, (((0,), (0,)), ((), ())), preferred_element_type=f32
    )
    return (projected, grad_down[None], grad_up[None])


def solution(mesh):
    in_specs = (
        P(("groups", "shard"), None),
        P("shard", None),
        P(("groups", "shard"), None),
        P("groups"),
        P("groups"),
        P(("groups", "shard"), None, None),
        P(("groups", "shard"), None, None),
        P(("groups", "shard"), None),
    )
    out_specs = (
        P(("groups", "shard"), None),
        P(("groups", "shard"), None, None),
        P(("groups", "shard"), None, None),
    )
    return jax.shard_map(local, mesh=mesh, in_specs=in_specs, out_specs=out_specs, check_vma=False)
```
